32 devices in a mesh: seq: 8 (over z, x), hid: 4 (over y, core).
Axes of the slice: x: 2, y: 2, z: 4, core: 2. Of those that a mesh axis runs over, the one named last changes fastest.
Arguments:
- tokens: bfloat16 [65536, 2048], P('seq', 'hid'), may hold values from -6 to 6
- cotangent: bfloat16 [65536, 2048], P('seq', 'hid'), may hold values from -6 to 6
- seq_first: bfloat16 [128, 512, 512], P('seq'), may hold values from -0.25 to 0.25
- seq_second: bfloat16 [512, 128, 128], P('seq'), may hold values from -0.5 to 0.5
- feat_first: bfloat16 [32, 64, 64], P('hid'), may hold values from -0.75 to 0.75
- feature_second_blocks: bfloat16 [64, 32, 32], P('hid'), may hold values from -1 to 1
- gate_scale: float32 [2048], P('hid'), may hold values from 0.5 to 2
- gate_bias: float32 [2048], P('hid'), may hold values from -3 to 3
Outputs:
- result: bfloat16 [65536, 2048], P('seq', 'hid')
- token_grad: bfloat16 [65536, 2048], P('seq', 'hid')
- first_grad: float32 [128, 512, 512], P('seq', 'hid')
- second_grad: float32 [512, 128, 128], P('seq', 'hid')
The draws below stay inside these ranges and needn't reach their ends.
All inputs are finite; a program needn't handle non-finite values.
Results may differ from the reference program's by a relative error of at most 0.0061.
Values may be sent and summed in bfloat16 or wider, within the bound.
A program may use at most 256 MiB of HBM per device.

```python
import jax
import jax.numpy as jnp

SB = 512
NB = 128
FB = 64
NF = 32
TOKENS = 65536
D = 2048


def levels(rng, shape, split, smallest, top_value):
    level, own = 1.0, jax.random.fold_in(rng, 6)
    for axis_at, shards_of in split:
        heights = jnp.exp(jax.random.uniform(jax.random.fold_in(own, axis_at), (shards_of,), jnp.float32, smallest / len(split), top_value / len(split)))
        level = level * jnp.repeat(heights, shape[axis_at] // shards_of).reshape([-1 if axis == axis_at else 1 for axis in range(len(shape))])
    return level


def bell_draw(key, extent, scale, bound, shards=(), held_as=jnp.bfloat16):
    factor_of = levels(key, extent, shards, -0.22, 0.18) if shards else 1.0
    values = jax.random.normal(key, extent, jnp.float32) * scale * factor_of
    return jnp.minimum(jnp.maximum(values, -bound), bound).astype(held_as)


def setup_inputs(seed: int = 0) -> dict:
    keys = jax.random.split(jax.random.key(seed), 9)
    return {
        "tokens": bell_draw(keys[0], (TOKENS, D), 1.0, 6.0, ((0, 8), (1, 4))),
        "cotangent": bell_draw(keys[1], (TOKENS, D), 1.0, 6.0, ((0, 8), (1, 4))),
        "seq_first": bell_draw(keys[2], (NB, SB, SB), SB ** -0.5, 0.25, ((0, 8),)),
        "seq_second": bell_draw(keys[3], (SB, NB, NB), NB ** -0.5, 0.5, ((0, 8),)),
        "feat_first": bell_draw(keys[4], (NF, FB, FB), FB ** -0.5, 0.75, ((0, 4),)),
        "feature_second_blocks": bell_draw(keys[5], (FB, NF, NF), NF ** -0.5, 1.0, ((0, 4),)),
        "gate_scale": jnp.clip(0.5 + 1.5 * jax.random.uniform(keys[6], (D,), jnp.float32) ** levels(keys[6], (D,), ((0, 4),), -0.2, 0.2), 0.5, 2.0),
        "gate_bias": bell_draw(keys[7], (D,), 1.0, 3.0, ((0, 4),), jnp.float32),
    }


def gelu_slope(value):
    normal_cdf = 0.5 * (1.0 + jax.scipy.special.erf(value * 0.7071067811865476))
    density = jnp.exp(-0.5 * value * value) * 0.3989422804014327
    return normal_cdf + value * density


def reference(tokens, cotangent, seq_first, seq_second, feat_first, feature_second_blocks, gate_scale, gate_bias):
    widened_input = jnp.float32
    half = jnp.bfloat16
    x_blocks = tokens.reshape(NB, SB, D).astype(widened_input)
    first = jnp.einsum('qkj,qjc->qkc', seq_first.astype(widened_input), x_blocks).astype(half)
    first_t = first.transpose(1, 0, 2).astype(widened_input)
    mixed_t = jnp.einsum('jab,jbc->jac', seq_second.astype(widened_input), first_t).astype(half)
    mixed = mixed_t.transpose(1, 0, 2).reshape(TOKENS, D).astype(widened_input)
    x_wide = tokens.astype(widened_input)
    gate = jax.nn.sigmoid(x_wide * gate_scale + gate_bias)
    hidden_state = (x_wide + gate * mixed).astype(half)
    panels = hidden_state.reshape(TOKENS, NF, FB).astype(widened_input)
    inner = jnp.einsum('bio,tbo->tbi', feat_first.astype(widened_input), panels).astype(half)
    activation_values = jax.nn.gelu(inner.astype(widened_input), approximate=False).astype(half)
    outer = jnp.einsum('ibd,tdi->tbi', feature_second_blocks.astype(widened_input), activation_values.astype(widened_input)).astype(half)
    result = (hidden_state.astype(widened_input) + outer.reshape(TOKENS, D).astype(widened_input)).astype(half)
    cot_panels = cotangent.reshape(TOKENS, NF, FB).astype(widened_input)
    activation_gradient = jnp.einsum('ibd,tbi->tdi', feature_second_blocks.astype(widened_input), cot_panels)
    d_inner = (activation_gradient * gelu_slope(inner.astype(widened_input))).astype(half)
    d_hidden = cotangent.astype(widened_input) + jnp.einsum('bio,tbi->tbo', feat_first.astype(widened_input), d_inner.astype(widened_input)).reshape(TOKENS, D)
    d_mixed = (d_hidden * gate).astype(half)
    d_mixed_t = d_mixed.reshape(NB, SB, D).transpose(1, 0, 2).astype(widened_input)
    d_first_t = jnp.einsum('jab,jac->jbc', seq_second.astype(widened_input), d_mixed_t).astype(half)
    second_grad = jnp.einsum('jac,jbc->jab', d_mixed_t, first_t)
    d_first = d_first_t.transpose(1, 0, 2).astype(widened_input)
    first_grad = jnp.einsum('qkc,qjc->qkj', d_first, x_blocks)
    seq_part = jnp.einsum('qkj,qkc->qjc', seq_first.astype(widened_input), d_first).reshape(TOKENS, D)
    local_part = d_hidden * (1.0 + gate_scale * gate * (1.0 - gate) * mixed)
    token_grad = (seq_part + local_part).astype(half)
    return result, token_grad, first_grad, second_grad
```

```python
import jax
import jax.numpy as jnp
from jax import lax
from jax.sharding import PartitionSpec as P

HALF = jnp.bfloat16
WIDE = jnp.float32


def dot(spec, left, right):
    return jnp.einsum(spec, left, right, preferred_element_type=WIDE)


def gelu_parts(value):
    normal_cdf = 0.5 * (1.0 + lax.erf(value * 0.7071067811865476))
    density = jnp.exp(-0.5 * value * value) * 0.3989422804014327
    return (value * normal_cdf).astype(HALF), normal_cdf + value * density


def swap_seq(value):
    return lax.all_to_all(value, "seq", split_axis=0, concat_axis=0, tiled=True)


def make_swap_hid(hid):
    pairwise = hid & (hid - 1) == 0 and hid <= 4

    def swap(value):
        lanes = value.shape[1] // hid
        if not pairwise:
            split = value.reshape(-1, hid, lanes).transpose(1, 0, 2)
            out = lax.all_to_all(split, "hid", split_axis=0, concat_axis=0, tiled=True)
            return out.transpose(1, 0, 2).reshape(value.shape)
        panels = [value[:, :lanes]]
        for step in range(1, hid):
            pairs = [(at, at ^ step) for at in range(hid)]
            panels.append(
                lax.ppermute(value[:, step * lanes : (step + 1) * lanes], "hid", pairs)
            )
        return jnp.concatenate(panels, axis=1)

    def order():
        at = jnp.arange(hid)
        return lax.axis_index("hid") ^ at if pairwise else at

    return swap, order


def on_device(seq, hid, tokens, cotangent, seq_first, seq_second, feat_first, feat_second, gate_scale, gate_bias):
    rows, width = tokens.shape
    blocks, block = seq_first.shape[:2]
    groups, group = feat_first.shape[:2]
    offsets_here, total_groups = feat_second.shape[:2]
    offsets = block // seq
    parts = 4 if offsets % 4 == 0 else 1
    step = offsets // parts
    part_rows = seq * blocks * step
    total_blocks = blocks * seq
    swap_hid, order = make_swap_hid(hid)
    panel = groups * offsets_here

    who = order()
    eye_b = jnp.eye(groups, dtype=HALF)
    w1 = feat_first.reshape(groups, hid, offsets_here, group)[:, who]
    into = jnp.einsum("bhio,bd->dohbi", w1, eye_b).reshape(width, hid * panel)
    back = into.T
    eye_i = jnp.eye(offsets_here, dtype=HALF)
    w2 = feat_second.reshape(offsets_here, hid, groups, hid, groups)[:, who][:, :, :, who]
    mix_out = jnp.einsum("ihbge,ij->gejhbi", w2, eye_i).reshape(hid * panel, hid * panel)
    mix_back = mix_out.T
    source = (
        jnp.arange(groups)[None, :, None] * group
        + who[:, None, None] * offsets_here
        + jnp.arange(offsets_here)[None, None, :]
    ).reshape(-1)
    spread = (source[:, None] == jnp.arange(width)[None, :]).astype(HALF)
    gather = spread.T

    def cut(value, length):
        return value.reshape(blocks, seq, parts, step, length)

    x_blocks = tokens.reshape(blocks, block, width)
    seq_rows = cut(seq_first, block)
    x_cut = cut(tokens, width)
    cot_cut = cut(cotangent, width)
    second_cut = seq_second.reshape(parts, step, total_blocks, total_blocks)

    def major(value):
        return value.transpose(1, 0, 2, 3).reshape(part_rows, width)

    weights = [seq_rows[:, :, p].reshape(blocks, seq * step, block) for p in range(parts)]
    strided, mixed, gates, hidden, inner = [], [], [], [], []
    for p in range(parts):
        first = dot("qkj,qjc->qkc", weights[p], x_blocks).astype(HALF)
        first = first.reshape(blocks, seq, step, width).transpose(1, 0, 2, 3)
        strided.append(swap_seq(first).reshape(total_blocks, step, width))
    for p in range(parts):
        here = dot("jab,bjc->ajc", second_cut[p], strided[p]).astype(HALF)
        mixed.append(swap_seq(here.reshape(seq, blocks, step, width)).reshape(part_rows, width))
    cots, cot_moved = [], []
    for p in range(parts):
        cots.append(major(cot_cut[:, :, p]))
        cot_moved.append(swap_hid(dot("tc,cd->td", cots[p], gather).astype(HALF)))
    results, moved, locals_, seconds = [], [], [], []
    for p in range(parts):
        x_wide = major(x_cut[:, :, p]).astype(WIDE)
        gate = jax.nn.sigmoid(x_wide * gate_scale + gate_bias)
        mixed_wide = mixed[p].astype(WIDE)
        state = (x_wide + gate * mixed_wide).astype(HALF)
        inner_moved = swap_hid(dot("tc,cd->td", state, into).astype(HALF))
        act, slope = gelu_parts(inner_moved.astype(WIDE))
        d_act = dot("td,ed->te", cot_moved[p], mix_out)
        d_inner = swap_hid((d_act * slope).astype(HALF))
        d_hidden = cots[p].astype(WIDE) + dot("td,dc->tc", d_inner, back)
        d_mixed = (d_hidden * gate).astype(HALF).reshape(seq, blocks, step, width)
        moved.append(swap_seq(d_mixed).reshape(total_blocks, step, width))
        locals_.append(
            (d_hidden * (1.0 + gate_scale * gate * (1.0 - gate) * mixed_wide)).astype(HALF)
        )
        outer = swap_hid(dot("td,de->te", act, mix_out).astype(HALF))
        outer = dot("td,dc->tc", outer, spread)
        results.append((state.astype(WIDE) + outer).astype(HALF))
    firsts, first_grads = [], []
    for p in range(parts):
        here = dot("jab,ajc->bjc", second_cut[p], moved[p]).astype(HALF)
        seconds.append(dot("ajc,bjc->jab", moved[p], strided[p]))
        back_here = swap_seq(here.reshape(seq, blocks, step, width))
        d_first = back_here.transpose(1, 0, 2, 3).reshape(blocks, seq * step, width)
        firsts.append(d_first)
        term = dot("qkc,qjc->qkj", d_first, x_blocks)
        term = lax.psum_scatter(term, "hid", scatter_dimension=1, tiled=True)
        first_grads.append(term.reshape(blocks, seq // hid, step, block))

    def join(values):
        stacked = jnp.stack([v.reshape(seq, blocks, step, width) for v in values])
        return stacked.transpose(2, 1, 0, 3, 4).reshape(rows, width)

    second_grad = lax.psum_scatter(
        jnp.concatenate(seconds, axis=0), "hid", scatter_dimension=1, tiled=True
    )
    seq_part = dot(
        "qkj,qkc->qjc", jnp.concatenate(weights, axis=1), jnp.concatenate(firsts, axis=1)
    ).reshape(rows, width)
    token_grad = (seq_part + join(locals_).astype(WIDE)).astype(HALF)
    first_grad = jnp.stack(first_grads, axis=2).reshape(blocks, block // hid, block)
    return (join(results), token_grad, first_grad, second_grad)


def solution(mesh):
    seq, hid = mesh.shape["seq"], mesh.shape["hid"]

    def body(*operands):
        return on_device(seq, hid, *operands)

    return jax.shard_map(
        body,
        mesh=mesh,
        in_specs=(
            P("seq", "hid"),
            P("seq", "hid"),
            P("seq", None, None),
            P("seq", None, None),
            P("hid", None, None),
            P("hid", None, None),
            P("hid"),
            P("hid"),
        ),
        out_specs=(P("seq", "hid"), P("seq", "hid"), P("seq", "hid", None), P("seq", "hid", None)),
        check_vma=False,
    )
```

```python
import jax
import jax.numpy as jnp
from jax import lax
from jax.experimental.layout import Layout, with_layout_constraint
from jax.sharding import PartitionSpec as P

HALF = jnp.bfloat16
WIDE = jnp.float32


def dot(spec, left, right):
    return jnp.einsum(spec, left, right, preferred_element_type=WIDE)


def gelu_parts(value):
    normal_cdf = 0.5 * (1.0 + lax.erf(value * 0.7071067811865476))
    density = jnp.exp(-0.5 * value * value) * 0.3989422804014327
    return (value * normal_cdf).astype(HALF), normal_cdf + value * density


def rowwise(value):
    return with_layout_constraint(value, Layout(major_to_minor=(0, 1)))


def swap_seq(value):
    return lax.all_to_all(value, "seq", split_axis=0, concat_axis=0, tiled=True)


def make_swap_hid(hid):
    pairwise = hid & (hid - 1) == 0 and hid <= 4

    def swap(value):
        lanes = value.shape[1] // hid
        if not pairwise:
            split = value.reshape(-1, hid, lanes).transpose(1, 0, 2)
            out = lax.all_to_all(split, "hid", split_axis=0, concat_axis=0, tiled=True)
            return out.transpose(1, 0, 2).reshape(value.shape)
        panels = [value[:, :lanes]]
        for step in range(1, hid):
            pairs = [(at, at ^ step) for at in range(hid)]
            panels.append(
                lax.ppermute(value[:, step * lanes : (step + 1) * lanes], "hid", pairs)
            )
        return jnp.concatenate(panels, axis=1)

    def order():
        at = jnp.arange(hid)
        return lax.axis_index("hid") ^ at if pairwise else at

    return swap, order


def on_device(seq, hid, tokens, cotangent, seq_first, seq_second, feat_first, feat_second, gate_scale, gate_bias):
    rows, width = tokens.shape
    blocks, block = seq_first.shape[:2]
    groups, group = feat_first.shape[:2]
    offsets_here, total_groups = feat_second.shape[:2]
    offsets = block // seq
    parts = 4 if offsets % 4 == 0 else 1
    step = offsets // parts
    part_rows = seq * blocks * step
    total_blocks = blocks * seq
    swap_hid, order = make_swap_hid(hid)
    panel = groups * offsets_here

    who = order()
    eye_b = jnp.eye(groups, dtype=HALF)
    w1 = feat_first.reshape(groups, hid, offsets_here, group)[:, who]
    into = jnp.einsum("bhio,bd->dohbi", w1, eye_b).reshape(width, hid * panel)
    back = into.T
    eye_i = jnp.eye(offsets_here, dtype=HALF)
    w2 = feat_second.reshape(offsets_here, hid, groups, hid, groups)[:, who][:, :, :, who]
    mix_out = jnp.einsum("ihbge,ij->gejhbi", w2, eye_i).reshape(hid * panel, hid * panel)
    mix_back = mix_out.T
    source = (
        jnp.arange(groups)[None, :, None] * group
        + who[:, None, None] * offsets_here
        + jnp.arange(offsets_here)[None, None, :]
    ).reshape(-1)
    spread = (source[:, None] == jnp.arange(width)[None, :]).astype(HALF)
    gather = spread.T

    def cut(value, length):
        return value.reshape(blocks, seq, parts, step, length)

    x_blocks = tokens.reshape(blocks, block, width)
    seq_rows = cut(seq_first, block)
    x_cut = cut(tokens, width)
    cot_cut = cut(cotangent, width)
    second_cut = seq_second.reshape(parts, step, total_blocks, total_blocks)

    def major(value):
        return value.transpose(1, 0, 2, 3).reshape(part_rows, width)

    weights = [seq_rows[:, :, p].reshape(blocks, seq * step, block) for p in range(parts)]
    sent = (seq, blocks, step, width)
    everyone = range(parts)
    held = {}

    def first_of(p):
        first = dot("qkj,qjc->qkc", weights[p], held["x"]).astype(HALF)
        held["send1", p] = first.reshape(blocks, seq, step, width).transpose(1, 0, 2, 3)

    def cot_of(p):
        held["cot", p] = rowwise(major(cot_cut[:, :, p]))
        panels = rowwise(dot("tc,cd->td", held["cot", p], gather).astype(HALF))
        held["cot_moved", p] = swap_hid(panels)

    def mix_of(p):
        strided = held["strided", p].reshape(total_blocks, step, width)
        here = dot("jab,bjc->ajc", second_cut[p], strided).astype(HALF)
        held["send2", p] = here.reshape(sent)

    def gate_of(p):
        x_wide = held["x", p].astype(WIDE)
        return x_wide, jax.nn.sigmoid(x_wide * gate_scale + gate_bias)

    def inner_of(p):
        held["x", p] = rowwise(major(x_cut[:, :, p]))
        x_wide, gate = gate_of(p)
        mixed_wide = rowwise(held["mixed", p].reshape(part_rows, width)).astype(WIDE)
        state = rowwise((x_wide + gate * mixed_wide).astype(HALF))
        held["state", p] = state
        panels = rowwise(dot("tc,cd->td", state, into).astype(HALF))
        held["inner", p] = swap_hid(panels)

    def d_inner_of(p):
        act, slope = gelu_parts(held["inner", p].astype(WIDE))
        held["act", p] = rowwise(act)
        d_act = dot("td,ed->te", held["cot_moved", p], mix_out)
        held["d_inner", p] = swap_hid(rowwise((d_act * slope).astype(HALF)))

    def d_mixed_of(p):
        d_hidden = held["cot", p].astype(WIDE) + dot("td,dc->tc", held["d_inner", p], back)
        x_wide, gate = gate_of(p)
        mixed_wide = held["mixed", p].reshape(part_rows, width).astype(WIDE)
        held["send3", p] = rowwise((d_hidden * gate).astype(HALF)).reshape(sent)
        local = d_hidden * (1.0 + gate_scale * gate * (1.0 - gate) * mixed_wide)
        held["local", p] = rowwise(local.astype(HALF))

    def result_of(p):
        panels = rowwise(dot("td,de->te", held["act", p], mix_out).astype(HALF))
        outer = dot("td,dc->tc", swap_hid(panels), spread)
        held["result", p] = rowwise((held["state", p].astype(WIDE) + outer).astype(HALF))

    def d_first_of(p):
        moved = held["moved", p].reshape(total_blocks, step, width)
        here = dot("jab,ajc->bjc", second_cut[p], moved).astype(HALF)
        held["send4", p] = here.reshape(sent)
        strided = held["strided", p].reshape(total_blocks, step, width)
        held["second", p] = dot("ajc,bjc->jab", moved, strided)

    def term_of(p):
        d_first = held["back", p].transpose(1, 0, 2, 3).reshape(blocks, seq * step, width)
        held["d_first", p] = d_first
        term = dot("qkc,qjc->qkj", d_first, x_blocks)
        term = lax.psum_scatter(term, "hid", scatter_dimension=1, tiled=True)
        held["grad", p] = term.reshape(blocks, seq // hid, step, block)

    moves = [
        (name, p)
        for name in (("send1", "strided"), ("send2", "mixed"), ("send3", "moved"), ("send4", "back"))
        for p in everyone
    ]
    plan = {n: [] for n in range(len(moves) + 1)}
    for p in everyone:
        if p:
            plan[p - 1].append((first_of, p))
        plan[p].append((cot_of, p))
        plan[parts if p == parts - 1 else p + 1].append((mix_of, p))
        after = parts + p
        plan[after + 1].append((inner_of, p))
        plan[after + 2].append((d_inner_of, p))
        plan[after + (3 if parts > 3 else 2)].append((d_mixed_of, p))
        plan[2 * parts + p + 1].append((d_first_of, p))
        plan[2 * parts + p + 2].append((result_of, p))
        plan[3 * parts + p + 1].append((term_of, p))
    held["x"] = x_blocks
    first_of(0)
    if parts == 1:
        held["strided", 0] = swap_seq(held["send1", 0])
        cot_of(0)
        mix_of(0)
        held["mixed", 0] = swap_seq(held["send2", 0])
        inner_of(0)
        d_inner_of(0)
        d_mixed_of(0)
        result_of(0)
        held["moved", 0] = swap_seq(held["send3", 0])
        d_first_of(0)
        held["back", 0] = swap_seq(held["send4", 0])
        term_of(0)
    else:
        for n, ((source_name, target), p) in enumerate(moves):
            names = [k for k in held if k[0] not in ("grad", "second")]
            for name, value in zip(names, lax.optimization_barrier([held[k] for k in names])):
                held[name] = value
            arrived = swap_seq(held[source_name, p])
            for work, q in plan[n]:
                work(q)
            held[target, p] = arrived
            del held[source_name, p]
        for work, q in plan[len(moves)]:
            work(q)

    firsts = [held["d_first", p] for p in everyone]
    first_grads = [held["grad", p] for p in everyone]
    seconds = [held["second", p] for p in everyone]
    locals_ = [held["local", p] for p in everyone]
    results = [held["result", p] for p in everyone]

    def join(values):
        stacked = jnp.stack([v.reshape(seq, blocks, step, width) for v in values])
        return stacked.transpose(2, 1, 0, 3, 4).reshape(rows, width)

    second_grad = lax.psum_scatter(
        jnp.concatenate(seconds, axis=0), "hid", scatter_dimension=1, tiled=True
    )
    seq_part = dot(
        "qkj,qkc->qjc", jnp.concatenate(weights, axis=1), jnp.concatenate(firsts, axis=1)
    ).reshape(rows, width)
    token_grad = (seq_part + join(locals_).astype(WIDE)).astype(HALF)
    first_grad = jnp.stack(first_grads, axis=2).reshape(blocks, block // hid, block)
    return (join(results), token_grad, first_grad, second_grad)


def solution(mesh):
    seq, hid = mesh.shape["seq"], mesh.shape["hid"]

    def body(*operands):
        return on_device(seq, hid, *operands)

    return jax.shard_map(
        body,
        mesh=mesh,
        in_specs=(
            P("seq", "hid"),
            P("seq", "hid"),
            P("seq", None, None),
            P("seq", None, None),
            P("hid", None, None),
            P("hid", None, None),
            P("hid"),
            P("hid"),
        ),
        out_specs=(P("seq", "hid"), P("seq", "hid"), P("seq", "hid", None), P("seq", "hid", None)),
        check_vma=False,
    )
```
